32 devices in a mesh: groups: 2 (over y), gx: 8 (over z, x), gy: 2 (over core).
Axes of the slice: x: 2, y: 2, z: 4, core: 2. Of those that a mesh axis runs over, the one named last changes fastest.
Arguments:
- offsets: int32 [6, 96, 128, 128], P('groups', 'gx', 'gy'), parts along dimension 0, may hold values from -4 to 3
- fractions: float32 [6, 96, 128, 128], P('groups', 'gx', 'gy'), parts along dimension 0, may hold values from 0 to 1
- masses: float32 [96, 128, 256], P('gx', 'gy', 'groups'), parts along dimension 2, may hold values from 0.3 to 3
- cotangents: float32 [6, 96, 128, 128], P('groups', 'gx', 'gy'), parts along dimension 0, may hold values from -6 to 6
- counts: int32 [192, 16], P(('groups', 'gx'), 'gy'), parts along dimension 0, may hold values from 64 to 1024, as said below
Outputs:
- forces: float32 [6, 160, 144, 128], P('groups', 'gx', 'gy'), parts along dimension 0
- density_adjoint: float32 [320, 144, 128], P(('groups', 'gx'), 'gy'), parts along dimension 0
The draws below stay inside these ranges and needn't reach their ends.
There are 2 independent parts, one for each index of `groups`. The reference program is written for one: setup_inputs(seed, part) draws one part's arguments, and reference() takes and returns one part's arrays. A program takes and returns all parts, laid end to end along the dimension named above; each array names one. Nothing has to cross between parts.
Inputs may be any that keep to these rules, and one draw needn't show every extreme that they name: counts[x, t] live particles in the tile of 8 x 128 lattice sites at plane x and rows 8 * t to 8 * t + 7; the live ones come first in the order y then z; at least one tile is full in every draw.
All inputs are finite; a program needn't handle non-finite values.
Results may differ from the reference program's by a relative error of at most 0.0039.
Values sent between devices are 32-bit elements; how exact they have to be, the bound alone decides.
A program may use at most 64 MiB of HBM per device.

```python
import math
import jax
import jax.numpy as jnp

CX = 12
CY = 64
CZ = 128
TROWS = 8
TILE = 1024
NX = 96
NY = 128
N_GX = 8
N_GY = 2


def draw_counts(key, part):
    key = jax.random.fold_in(key, 11)
    key_level, key_base, key_full = jax.random.split(key, 3)
    slabs = NX // CX
    level = jax.random.randint(key_level, (slabs,), 1, 5)
    base = jax.random.randint(key_base, (NX, NY // TROWS), TILE // 4, TILE + 1)
    spread = jnp.repeat(level, CX)[:, None]
    counts = spread * base // 4
    filled = jax.random.randint(key_full, (NX, NY // TROWS), 0, 8) == 0
    counts = jnp.where(filled & (spread == 4), TILE, counts)
    counts = counts.at[0, 0].set(TILE)
    return counts.astype(jnp.int32)


def with_ends(result, key, low, largest):
    dims = result.shape
    spot = [jax.random.randint(jax.random.fold_in(key, axis), (), 0, dims[axis]) for axis in range(len(dims))]
    result = result.at[tuple(spot)].set(low)
    longest = dims.index(max(dims))
    spot[longest] = (spot[longest] + 1) % dims[longest]
    return result.at[tuple(spot)].set(largest)


def level_of(own_key, extent, cuts, low, largest):
    loudness, own = 1.0, jax.random.fold_in(own_key, 6)
    for position, blocks in cuts:
        heights = jnp.exp(jax.random.uniform(jax.random.fold_in(own, position), (blocks,), jnp.float32, low / len(cuts), largest / len(cuts)))
        loudness = loudness * jnp.repeat(heights, extent[position] // blocks).reshape([-1 if axis == position else 1 for axis in range(len(extent))])
    return loudness


def normal_values(key, extent, deviation, most, shards=(), held_as=jnp.bfloat16):
    factor_of = level_of(key, extent, shards, -0.22, 0.18) if shards else 1.0
    array = jax.random.normal(key, extent, jnp.float32) * deviation * factor_of
    return jnp.minimum(jnp.maximum(array, -most), most).astype(held_as)


def setup_inputs(seed: int = 0, part: int = 0) -> dict:
    seeds = jax.random.split(jax.random.key(seed), 6)
    part_splits = jax.random.split(jax.random.fold_in(seeds[5], part), 6)
    offsets = with_ends(jax.random.randint(part_splits[0], (3, NX, NY, CZ), -4, 4), jax.random.fold_in(part_splits[0], 1), -4, 3).astype(jnp.int32)
    fractions = jnp.clip(1.0 * jax.random.uniform(part_splits[1], (3, NX, NY, CZ), jnp.float32) ** level_of(part_splits[1], (3, NX, NY, CZ), ((1, 8), (2, 2)), -0.2, 0.2), 0.0, 1.0)
    masses = jnp.clip(jnp.exp(math.log(3.0) - 2.3025851 * jax.random.uniform(part_splits[2], (NX, NY, CZ), jnp.float32) ** level_of(part_splits[2], (NX, NY, CZ), ((0, 8), (1, 2)), -0.2, 0.2)), 0.3, 3.0)
    cotangents = normal_values(part_splits[3], (3, NX, NY, CZ), 1.0, 6.0, ((1, 8), (2, 2)), jnp.float32)
    counts = draw_counts(jax.random.fold_in(jax.random.fold_in(seeds[5], part), 71), part)
    return dict(offsets=offsets, fractions=fractions, masses=masses, cotangents=cotangents, counts=counts)


def central(field, axis):
    return 0.5 * (jnp.roll(field, -1, axis) - jnp.roll(field, 1, axis))


def reference(offsets, fractions, masses, cotangents, counts):
    rows_y = jnp.arange(NY, dtype=jnp.int32)
    depth_z = jnp.arange(CZ, dtype=jnp.int32)
    places = ((rows_y % TROWS)[:, None] * CZ + depth_z[None, :]).astype(jnp.int32)
    tile_counts = counts[:, rows_y // TROWS]
    live = (places[None, :, :] < tile_counts[:, :, None]).astype(jnp.float32)
    values = jnp.concatenate([masses[None], cotangents], 0) * live[None]
    base_x = jnp.arange(NX, dtype=jnp.int32)[:, None, None] + offsets[0]
    base_y = rows_y[None, :, None] + offsets[1]
    base_z = depth_z[None, None, :] + offsets[2]
    fields = jnp.zeros((4, NX * NY * CZ), jnp.float32)
    for corner_a in range(2):
        weight_x = fractions[0] if corner_a else 1.0 - fractions[0]
        cell_x = (base_x + corner_a) % NX
        for corner_b in range(2):
            weight_y = fractions[1] if corner_b else 1.0 - fractions[1]
            cell_y = (base_y + corner_b) % NY
            left = ((weight_x * weight_y)[None] * values).astype(jnp.bfloat16).astype(jnp.float32)
            for corner_c in range(2):
                weight_z = fractions[2] if corner_c else 1.0 - fractions[2]
                right = weight_z.astype(jnp.bfloat16).astype(jnp.float32)
                cell_z = (base_z + corner_c) % CZ
                flat = ((cell_x * NY + cell_y) * CZ + cell_z).astype(jnp.int32).reshape(-1)
                terms = (left * right[None]).reshape(4, -1)
                fields = fields.at[:, flat].add(terms)
    fields = fields.reshape(4, NX, NY, CZ)
    density = fields[0]
    full_forces = -jnp.stack([central(density, 0), central(density, 1), central(density, 2)])
    full_adjoint = central(fields[1], 0) + central(fields[2], 1) + central(fields[3], 2)
    pick_x = ((jnp.arange(N_GX, dtype=jnp.int32)[:, None] * CX + jnp.arange(CX + 8, dtype=jnp.int32)[None, :] - 4) % NX).reshape(-1)
    pick_y = ((jnp.arange(N_GY, dtype=jnp.int32)[:, None] * CY + jnp.arange(CY + 8, dtype=jnp.int32)[None, :] - 4) % NY).reshape(-1)
    forces = jnp.take(jnp.take(full_forces, pick_x, axis=1), pick_y, axis=2)
    density_adjoint = jnp.take(jnp.take(full_adjoint, pick_x, axis=0), pick_y, axis=1)
    return forces, density_adjoint
```

```python
import functools

import jax
import jax.numpy as jnp
from jax import lax
from jax.experimental import pallas as pl
from jax.experimental.pallas import tpu as pltpu
from jax.sharding import PartitionSpec as P

TROWS = 8
REACH = 9
WINDOW = 16
PAIR = 2
EDGE = 8


def deposit_kernel(counts_ref, off_ref, frac_ref, mass_ref, cot_ref, out_ref, mesh, prep, left, right):
    x = pl.program_id(0)
    width_y, depth = mass_ref.shape[1:]
    planes, rows_all = mesh.shape[1:3]
    span = PAIR * depth

    @pl.when(x == 0)
    def _():
        mesh[...] = jnp.zeros_like(mesh)

    sub = lax.broadcasted_iota(jnp.int32, (TROWS, depth), 0)
    lane = lax.broadcasted_iota(jnp.int32, (TROWS, depth), 1)
    window_y = lax.broadcasted_iota(jnp.int32, (WINDOW, depth), 0).astype(jnp.float32)
    window_z = lax.broadcasted_iota(jnp.int32, (depth, depth), 0).astype(jnp.float32).astype(jnp.bfloat16)
    zero16 = jnp.zeros((depth, depth), jnp.bfloat16)

    def spread(index, row, count):
        return jnp.broadcast_to(prep[index, row : row + 1, :], (count, depth))

    def build(pair):
        for row in range(PAIR * pair, PAIR * pair + PAIR):
            cols = slice(row * depth, row * depth + depth)
            cell = spread(13, row, WINDOW)
            upper = spread(14, row, WINDOW)
            weight_y = jnp.where(
                window_y == cell, 1.0 - upper, jnp.where(window_y == cell + 1.0, upper, 0.0)
            )
            tops = [weight_y * spread(9 + k, row, WINDOW) for k in range(4)]
            for dx in range(REACH):
                weight_x = spread(dx, row, WINDOW)
                for k in range(4):
                    at = (k * REACH + dx) * WINDOW
                    left[at : at + WINDOW, cols] = (weight_x * tops[k]).astype(jnp.bfloat16)
            low = spread(15, row, depth).astype(jnp.bfloat16)
            high = spread(16, row, depth).astype(jnp.bfloat16)
            one = spread(17, row, depth).astype(jnp.bfloat16)
            two = spread(18, row, depth).astype(jnp.bfloat16)
            right[:, cols] = jnp.where(
                window_z == low, one, jnp.where(window_z == high, two, zero16)
            )

    def tile(t, carry):
        rows = pl.ds(pl.multiple_of(t * TROWS, TROWS), TROWS)
        count = counts_ref[x, t]
        live = sub * depth + lane < count
        shift_x = off_ref[0, 0, rows, :] + 4
        frac_x = frac_ref[0, 0, rows, :]
        for dx in range(REACH):
            prep[dx] = jnp.where(
                shift_x == dx, 1.0 - frac_x, jnp.where(shift_x == dx - 1, frac_x, 0.0)
            )
        prep[9] = jnp.where(live, mass_ref[0, rows, :], 0.0)
        for k in range(3):
            prep[10 + k] = jnp.where(live, cot_ref[k, 0, rows, :], 0.0)
        prep[13] = (off_ref[1, 0, rows, :] + sub + 4).astype(jnp.float32)
        prep[14] = frac_ref[1, 0, rows, :]
        lower = lane + off_ref[2, 0, rows, :]
        prep[15] = ((lower + depth) % depth).astype(jnp.float32)
        prep[16] = ((lower + (depth + 1)) % depth).astype(jnp.float32)
        frac_z = frac_ref[2, 0, rows, :]
        prep[17] = 1.0 - frac_z
        prep[18] = frac_z

        def work(pairs):
            for pair in range(pairs):
                build(pair)
            product = lax.dot_general(
                left[:, : pairs * span],
                right[:, : pairs * span],
                (((1,), (1,)), ((), ())),
                preferred_element_type=jnp.float32,
            ).reshape(4, REACH, WINDOW, depth)
            place = (slice(None), pl.ds(x + 2, REACH), pl.ds(pl.multiple_of(t * TROWS + EDGE, TROWS), WINDOW), slice(None))
            mesh[place] = mesh[place] + product

        most = TROWS // PAIR
        for pairs in range(1, most + 1):
            @pl.when((count > span * (pairs - 1)) & (count <= span * pairs))
            def _():
                work(pairs)

        return carry

    lax.fori_loop(0, width_y // TROWS, tile, 0)

    @pl.when(x == pl.num_programs(0) - 1)
    def _():
        def finish(p, carry):
            out_ref[0, p] = mesh[0, p + 1]
            side = mesh[2, p + 1]
            along = mesh[3, p + 1]
            out_ref[1, p] = 0.5 * (
                (mesh[1, p + 2] - mesh[1, p])
                + (pltpu.roll(side, rows_all - 1, 0) - pltpu.roll(side, 1, 0))
                + (pltpu.roll(along, depth - 1, 1) - pltpu.roll(along, 1, 1))
            )
            return carry

        lax.fori_loop(0, planes - 2, finish, 0)


def deposit(offsets, fractions, masses, cotangents, counts):
    width_x, width_y, depth = masses.shape
    rows_all = width_y + 8 + 2 * EDGE
    planes = width_x + 12
    triple = pl.BlockSpec((3, 1, width_y, depth), lambda i: (0, i, 0, 0))
    return pl.pallas_call(
        deposit_kernel,
        grid=(width_x,),
        out_shape=jax.ShapeDtypeStruct((2, planes - 2, rows_all, depth), jnp.float32),
        in_specs=[
            pl.BlockSpec(memory_space=pltpu.SMEM),
            triple,
            triple,
            pl.BlockSpec((1, width_y, depth), lambda i: (i, 0, 0)),
            triple,
        ],
        out_specs=pl.BlockSpec((2, planes - 2, rows_all, depth), lambda i: (0, 0, 0, 0)),
        scratch_shapes=[
            pltpu.VMEM((4, planes, rows_all, depth), jnp.float32),
            pltpu.VMEM((19, TROWS, depth), jnp.float32),
            pltpu.VMEM((4 * REACH * WINDOW, TROWS * depth), jnp.bfloat16),
            pltpu.VMEM((depth, TROWS * depth), jnp.bfloat16),
        ],
        compiler_params=pltpu.CompilerParams(vmem_limit_bytes=40 << 20),
        name="deposit",
    )(counts, offsets, fractions, masses, cotangents)


def from_behind(block, axis, distance):
    devices = range(lax.axis_size(axis))
    route = [((i - distance) % len(devices), i) for i in devices]
    return lax.ppermute(block, axis, route)


def shards(offsets, fractions, masses, cotangents, counts):
    width_x, width_y, depth = masses.shape
    raw = deposit(offsets, fractions, masses, cotangents, counts)
    below = from_behind(raw[:, :, width_y + 7 : width_y + 17], "gy", 1)
    above = from_behind(raw[:, :, 7:17], "gy", -1)
    rows = raw[:, :, 7 : width_y + 17]
    pad = ((0, 0), (0, 0), (0, width_y), (0, 0)), ((0, 0), (0, 0), (width_y, 0), (0, 0))
    rows = rows + jnp.pad(below, pad[0]) + jnp.pad(above, pad[1])
    behind = from_behind(rows[:, width_x:], "gx", 1)
    ahead = from_behind(rows[:, :10], "gx", -1)
    pad = ((0, 0), (0, width_x), (0, 0), (0, 0)), ((0, 0), (width_x, 0), (0, 0), (0, 0))
    full = rows + jnp.pad(behind, pad[0]) + jnp.pad(ahead, pad[1])
    density = full[0]
    force_x = -0.5 * (density[2:, 1:-1] - density[:-2, 1:-1])
    force_y = -0.5 * (density[1:-1, 2:] - density[1:-1, :-2])
    force_z = -0.5 * (jnp.roll(density, -1, 2) - jnp.roll(density, 1, 2))[1:-1, 1:-1]
    forces = jnp.stack([force_x, force_y[:, :], force_z])
    return forces[:, :, : width_y + 8], full[1, 1:-1, 1 : width_y + 9]


def solution(mesh):
    in_specs = (
        P("groups", "gx", "gy", None),
        P("groups", "gx", "gy", None),
        P("gx", "gy", "groups"),
        P("groups", "gx", "gy", None),
        P(("groups", "gx"), "gy"),
    )
    out_specs = (P("groups", "gx", "gy", None), P(("groups", "gx"), "gy", None))
    return jax.shard_map(shards, mesh=mesh, in_specs=in_specs, out_specs=out_specs, check_vma=False)
```

```python
import functools

import jax
import jax.numpy as jnp
from jax import lax
from jax.experimental import pallas as pl
from jax.experimental.pallas import tpu as pltpu
from jax.sharding import PartitionSpec as P

TROWS = 8
REACH = 9
WINDOW = 16
PAIR = 4
EDGE = 8


def deposit_kernel(counts_ref, off_ref, frac_ref, val_ref, out_ref, mesh, prep, left_a, left_b, right_a, right_b):
    x = pl.program_id(0)
    fields, _, width_y, depth = val_ref.shape
    planes, rows_all = mesh.shape[1:3]
    tiles = width_y // TROWS
    span = PAIR * depth

    @pl.when(x == 0)
    def _():
        mesh[...] = jnp.zeros_like(mesh)
        prep[:, width_y:, :] = jnp.zeros((prep.shape[0], TROWS, depth), jnp.float32)

    sub = lax.broadcasted_iota(jnp.int32, (TROWS, depth), 0)
    lane = lax.broadcasted_iota(jnp.int32, (TROWS, depth), 1)
    window_y = lax.broadcasted_iota(jnp.int32, (WINDOW, depth), 0).astype(jnp.float32)
    window_z = lax.broadcasted_iota(jnp.int32, (depth, depth), 0).astype(jnp.float32).astype(jnp.bfloat16)
    zero16 = jnp.zeros((depth, depth), jnp.bfloat16)

    def prepare(t, carry):
        rows = pl.ds(pl.multiple_of(t * TROWS, TROWS), TROWS)
        live = sub * depth + lane < counts_ref[x, t]
        shift_x = off_ref[0, 0, rows, :] + 4
        frac_x = frac_ref[0, 0, rows, :]
        for dx in range(REACH):
            prep[dx, rows, :] = jnp.where(
                shift_x == dx, 1.0 - frac_x, jnp.where(shift_x == dx - 1, frac_x, 0.0)
            )
        for k in range(fields):
            prep[9 + k, rows, :] = jnp.where(live, val_ref[k, 0, rows, :], 0.0)
        prep[13, rows, :] = (off_ref[1, 0, rows, :] + sub + 4).astype(jnp.float32)
        prep[14, rows, :] = frac_ref[1, 0, rows, :]
        lower = lane + off_ref[2, 0, rows, :]
        prep[15, rows, :] = (lower & (depth - 1)).astype(jnp.float32)
        prep[16, rows, :] = ((lower + 1) & (depth - 1)).astype(jnp.float32)
        frac_z = frac_ref[2, 0, rows, :]
        prep[17, rows, :] = 1.0 - frac_z
        prep[18, rows, :] = frac_z
        return carry

    lax.fori_loop(0, tiles, prepare, 0)

    def build(item, left, right):
        first = item[2]
        for row in range(PAIR):
            def spread(index, count):
                return jnp.broadcast_to(prep[index, pl.ds(first + row, 1), :], (count, depth))

            cols = slice(row * depth, row * depth + depth)
            cell = spread(13, WINDOW)
            upper = spread(14, WINDOW)
            weight_y = jnp.where(
                window_y == cell, 1.0 - upper, jnp.where(window_y == cell + 1.0, upper, 0.0)
            )
            tops = [weight_y * spread(9 + k, WINDOW) for k in range(fields)]
            for dx in range(REACH):
                weight_x = spread(dx, WINDOW)
                for k in range(fields):
                    at = (k * REACH + dx) * WINDOW
                    left[at : at + WINDOW, cols] = (weight_x * tops[k]).astype(jnp.bfloat16)
            low = spread(15, depth).astype(jnp.bfloat16)
            high = spread(16, depth).astype(jnp.bfloat16)
            one = spread(17, depth).astype(jnp.bfloat16)
            two = spread(18, depth).astype(jnp.bfloat16)
            right[:, cols] = jnp.where(
                window_z == low, one, jnp.where(window_z == high, two, zero16)
            )

    def add(item, left, right):
        product = lax.dot_general(
            left[...], right[...], (((1,), (1,)), ((), ())), preferred_element_type=jnp.float32
        ).reshape(fields, REACH, WINDOW, depth)
        rows = pl.ds(pl.multiple_of(item[0] * TROWS + EDGE, TROWS), WINDOW)
        place = (slice(None), pl.ds(x + 2, REACH), rows, slice(None))
        mesh[place] = mesh[place] + product

    def after(item):
        t, part, _ = item
        more = (part + 1) * span < counts_ref[x, t]
        over = jnp.logical_and(jnp.logical_not(more), t == tiles - 1)
        ended = jnp.logical_or(over, item[2] == width_y)
        nt = jnp.where(more, t, jnp.minimum(t + 1, tiles - 1))
        part = jnp.where(more, part + 1, 0)
        return nt, part, jnp.where(ended, width_y, nt * TROWS + part * PAIR)

    total = lax.fori_loop(
        0, tiles, lambda t, n: n + jnp.maximum((counts_ref[x, t] + (span - 1)) // span, 1), 0
    )
    zero = jnp.int32(0)
    start = (zero, zero, zero)
    build(start, left_a, right_a)

    def two_items(j, item):
        second = after(item)
        build(second, left_b, right_b)
        add(item, left_a, right_a)
        third = after(second)
        build(third, left_a, right_a)
        add(second, left_b, right_b)
        return third

    lax.fori_loop(0, (total + 1) // 2, two_items, start)

    @pl.when(x == pl.num_programs(0) - 1)
    def _():
        def finish(p, carry):
            if fields == 1:
                out_ref[p] = mesh[0, p + 1]
            else:
                side = mesh[1, p + 1]
                along = mesh[2, p + 1]
                out_ref[p] = 0.5 * (
                    (mesh[0, p + 2] - mesh[0, p])
                    + (pltpu.roll(side, rows_all - 1, 0) - pltpu.roll(side, 1, 0))
                    + (pltpu.roll(along, depth - 1, 1) - pltpu.roll(along, 1, 1))
                )
            return carry

        lax.fori_loop(0, planes - 2, finish, 0)


def deposit(offsets, fractions, values, counts, name):
    fields, width_x, width_y, depth = values.shape
    rows_all = width_y + 8 + 2 * EDGE
    planes = width_x + 12
    triple = pl.BlockSpec((3, 1, width_y, depth), lambda i: (0, i, 0, 0))
    lefts = pltpu.VMEM((fields * REACH * WINDOW, PAIR * depth), jnp.bfloat16)
    rights = pltpu.VMEM((depth, PAIR * depth), jnp.bfloat16)
    return pl.pallas_call(
        deposit_kernel,
        grid=(width_x,),
        out_shape=jax.ShapeDtypeStruct((planes - 2, rows_all, depth), jnp.float32),
        in_specs=[
            pl.BlockSpec(memory_space=pltpu.SMEM),
            triple,
            triple,
            pl.BlockSpec((fields, 1, width_y, depth), lambda i: (0, i, 0, 0)),
        ],
        out_specs=pl.BlockSpec((planes - 2, rows_all, depth), lambda i: (0, 0, 0)),
        scratch_shapes=[
            pltpu.VMEM((fields, planes, rows_all, depth), jnp.float32),
            pltpu.VMEM((19, width_y + TROWS, depth), jnp.float32),
            lefts,
            lefts,
            rights,
            rights,
        ],
        compiler_params=pltpu.CompilerParams(vmem_limit_bytes=56 << 20),
        cost_estimate=pl.CostEstimate(
            flops=2 * values.size * REACH * WINDOW * depth, bytes_accessed=40 * values.size, transcendentals=0
        ),
        name=name,
    )(counts, offsets, fractions, values)


def from_behind(block, axis, distance):
    devices = range(lax.axis_size(axis))
    route = [((i - distance) % len(devices), i) for i in devices]
    return lax.ppermute(block, axis, route)


def join_y(raw, width_y):
    below = from_behind(raw[:, width_y + 7 : width_y + 17], "gy", 1)
    above = from_behind(raw[:, 7:17], "gy", -1)
    return (
        raw[:, 7 : width_y + 17]
        + jnp.pad(below, ((0, 0), (0, width_y), (0, 0)))
        + jnp.pad(above, ((0, 0), (width_y, 0), (0, 0)))
    )


def send_x(field, width_x, low, high):
    behind = from_behind(field[width_x + low : width_x + low + 9], "gx", 1)
    ahead = from_behind(field[high : high + 9], "gx", -1)
    return behind, ahead


def join_x(field, behind, ahead, width_x, low, high):
    return (
        field
        + jnp.pad(behind, ((low, width_x + 1 - low), (0, 0), (0, 0)))
        + jnp.pad(ahead, ((width_x + high, 1 - high), (0, 0), (0, 0)))
    )


def shards(offsets, fractions, masses, cotangents, counts):
    width_x, width_y, depth = masses.shape
    raw = deposit(offsets, fractions, masses[None], counts, "deposit_masses")
    rows = join_y(raw, width_y)
    rows, cotangents = lax.optimization_barrier((rows, cotangents))
    sent = send_x(rows, width_x, 0, 1)
    raw = deposit(offsets, fractions, cotangents, counts, "deposit_cotangents")
    raw, sent = lax.optimization_barrier((raw, sent))
    density = join_x(rows, *sent, width_x, 0, 1)
    parts = join_y(raw, width_y)[:, 1 : width_y + 9]
    adjoint = join_x(parts, *send_x(parts, width_x, 1, 0), width_x, 1, 0)
    force_x = -0.5 * (density[2:, 1:-1] - density[:-2, 1:-1])
    force_y = -0.5 * (density[1:-1, 2:] - density[1:-1, :-2])
    force_z = -0.5 * (jnp.roll(density, -1, 2) - jnp.roll(density, 1, 2))[1:-1, 1:-1]
    forces = jnp.stack([force_x, force_y, force_z])
    return forces, adjoint[1:-1]


def solution(mesh):
    in_specs = (
        P("groups", "gx", "gy", None),
        P("groups", "gx", "gy", None),
        P("gx", "gy", "groups"),
        P("groups", "gx", "gy", None),
        P(("groups", "gx"), "gy"),
    )
    out_specs = (P("groups", "gx", "gy", None), P(("groups", "gx"), "gy", None))
    return jax.shard_map(shards, mesh=mesh, in_specs=in_specs, out_specs=out_specs, check_vma=False)
```

```python
import functools

import jax
import jax.numpy as jnp
from jax import lax
from jax.experimental import pallas as pl
from jax.experimental.pallas import tpu as pltpu
from jax.sharding import PartitionSpec as P

TROWS = 8
REACH = 9
WINDOW = 16
PAIR = 4
EDGE = 8


def deposit_kernel(counts_ref, off_ref, frac_ref, mass_ref, cot_ref, out_ref, mesh, prep, left_a, left_b, right_a, right_b):
    x = pl.program_id(0)
    width_y, depth = mass_ref.shape[1:]
    planes, rows_all = mesh.shape[1:3]
    tiles = width_y // TROWS
    span = PAIR * depth

    @pl.when(x == 0)
    def _():
        mesh[...] = jnp.zeros_like(mesh)
        prep[:, width_y:, :] = jnp.zeros((prep.shape[0], TROWS, depth), jnp.float32)

    sub = lax.broadcasted_iota(jnp.int32, (TROWS, depth), 0)
    lane = lax.broadcasted_iota(jnp.int32, (TROWS, depth), 1)
    window_y = lax.broadcasted_iota(jnp.int32, (WINDOW, depth), 0).astype(jnp.float32)
    window_z = lax.broadcasted_iota(jnp.int32, (depth, depth), 0).astype(jnp.float32).astype(jnp.bfloat16)
    zero16 = jnp.zeros((depth, depth), jnp.bfloat16)

    def prepare(t, carry):
        rows = pl.ds(pl.multiple_of(t * TROWS, TROWS), TROWS)
        live = sub * depth + lane < counts_ref[x, t]
        shift_x = off_ref[0, 0, rows, :] + 4
        frac_x = frac_ref[0, 0, rows, :]
        for dx in range(REACH):
            prep[dx, rows, :] = jnp.where(
                shift_x == dx, 1.0 - frac_x, jnp.where(shift_x == dx - 1, frac_x, 0.0)
            )
        prep[9, rows, :] = jnp.where(live, mass_ref[0, rows, :], 0.0)
        for k in range(3):
            prep[10 + k, rows, :] = jnp.where(live, cot_ref[k, 0, rows, :], 0.0)
        prep[13, rows, :] = (off_ref[1, 0, rows, :] + sub + 4).astype(jnp.float32)
        prep[14, rows, :] = frac_ref[1, 0, rows, :]
        lower = lane + off_ref[2, 0, rows, :]
        prep[15, rows, :] = (lower & (depth - 1)).astype(jnp.float32)
        prep[16, rows, :] = ((lower + 1) & (depth - 1)).astype(jnp.float32)
        frac_z = frac_ref[2, 0, rows, :]
        prep[17, rows, :] = 1.0 - frac_z
        prep[18, rows, :] = frac_z
        return carry

    lax.fori_loop(0, tiles, prepare, 0)

    def build(item, left, right):
        first = item[2]
        for row in range(PAIR):
            def spread(index, count):
                return jnp.broadcast_to(prep[index, pl.ds(first + row, 1), :], (count, depth))

            cols = slice(row * depth, row * depth + depth)
            cell = spread(13, WINDOW)
            upper = spread(14, WINDOW)
            weight_y = jnp.where(
                window_y == cell, 1.0 - upper, jnp.where(window_y == cell + 1.0, upper, 0.0)
            )
            tops = [weight_y * spread(9 + k, WINDOW) for k in range(4)]
            for dx in range(REACH):
                weight_x = spread(dx, WINDOW)
                for k in range(4):
                    at = (k * REACH + dx) * WINDOW
                    left[at : at + WINDOW, cols] = (weight_x * tops[k]).astype(jnp.bfloat16)
            low = spread(15, depth).astype(jnp.bfloat16)
            high = spread(16, depth).astype(jnp.bfloat16)
            one = spread(17, depth).astype(jnp.bfloat16)
            two = spread(18, depth).astype(jnp.bfloat16)
            right[:, cols] = jnp.where(
                window_z == low, one, jnp.where(window_z == high, two, zero16)
            )

    def add(item, left, right):
        rows = pl.ds(pl.multiple_of(item[0] * TROWS + EDGE, TROWS), WINDOW)
        held = right[...]
        step = 4 // 2
        for k in range(0, 4, step):
            product = lax.dot_general(
                left[k * REACH * WINDOW : (k + step) * REACH * WINDOW, :], held, (((1,), (1,)), ((), ())), preferred_element_type=jnp.float32
            ).reshape(step, REACH, WINDOW, depth)
            place = (slice(k, k + step), pl.ds(x + 2, REACH), rows, slice(None))
            mesh[place] = mesh[place] + product

    def after(item):
        t, part, _ = item
        more = (part + 1) * span < counts_ref[x, t]
        over = jnp.logical_and(jnp.logical_not(more), t == tiles - 1)
        ended = jnp.logical_or(over, item[2] == width_y)
        nt = jnp.where(more, t, jnp.minimum(t + 1, tiles - 1))
        part = jnp.where(more, part + 1, 0)
        return nt, part, jnp.where(ended, width_y, nt * TROWS + part * PAIR)

    total = lax.fori_loop(
        0, tiles, lambda t, n: n + jnp.maximum((counts_ref[x, t] + (span - 1)) // span, 1), 0
    )
    zero = jnp.int32(0)
    start = (zero, zero, zero)
    build(start, left_a, right_a)

    def two_items(j, item):
        second = after(item)
        build(second, left_b, right_b)
        add(item, left_a, right_a)
        third = after(second)
        build(third, left_a, right_a)
        add(second, left_b, right_b)
        return third

    lax.fori_loop(0, (total + 1) // 2, two_items, start)

    @pl.when(x == pl.num_programs(0) - 1)
    def _():
        def finish(p, carry):
            out_ref[0, p] = mesh[0, p + 1]
            side = mesh[2, p + 1]
            along = mesh[3, p + 1]
            out_ref[1, p] = 0.5 * (
                (mesh[1, p + 2] - mesh[1, p])
                + (pltpu.roll(side, rows_all - 1, 0) - pltpu.roll(side, 1, 0))
                + (pltpu.roll(along, depth - 1, 1) - pltpu.roll(along, 1, 1))
            )
            return carry

        lax.fori_loop(0, planes - 2, finish, 0)


def deposit(offsets, fractions, masses, cotangents, counts):
    width_x, width_y, depth = masses.shape
    rows_all = width_y + 8 + 2 * EDGE
    planes = width_x + 12
    triple = pl.BlockSpec((3, 1, width_y, depth), lambda i: (0, i, 0, 0))
    return pl.pallas_call(
        deposit_kernel,
        grid=(width_x,),
        out_shape=jax.ShapeDtypeStruct((2, planes - 2, rows_all, depth), jnp.float32),
        in_specs=[
            pl.BlockSpec(memory_space=pltpu.SMEM),
            triple,
            triple,
            pl.BlockSpec((1, width_y, depth), lambda i: (i, 0, 0)),
            triple,
        ],
        out_specs=pl.BlockSpec((2, planes - 2, rows_all, depth), lambda i: (0, 0, 0, 0)),
        scratch_shapes=[
            pltpu.VMEM((4, planes, rows_all, depth), jnp.float32),
            pltpu.VMEM((19, width_y + TROWS, depth), jnp.float32),
            pltpu.VMEM((4 * REACH * WINDOW, PAIR * depth), jnp.bfloat16),
            pltpu.VMEM((4 * REACH * WINDOW, PAIR * depth), jnp.bfloat16),
            pltpu.VMEM((depth, PAIR * depth), jnp.bfloat16),
            pltpu.VMEM((depth, PAIR * depth), jnp.bfloat16),
        ],
        compiler_params=pltpu.CompilerParams(vmem_limit_bytes=56 << 20),
        name="deposit",
    )(counts, offsets, fractions, masses, cotangents)


def from_behind(block, axis, distance):
    devices = range(lax.axis_size(axis))
    route = [((i - distance) % len(devices), i) for i in devices]
    return lax.ppermute(block, axis, route)


def send_x(field, width_x, low, high):
    behind = from_behind(field[width_x + low : width_x + low + 9], "gx", 1)
    ahead = from_behind(field[high : high + 9], "gx", -1)
    return behind, ahead


def join_x(field, behind, ahead, width_x, low, high):
    return (
        field
        + jnp.pad(behind, ((low, width_x + 1 - low), (0, 0), (0, 0)))
        + jnp.pad(ahead, ((width_x + high, 1 - high), (0, 0), (0, 0)))
    )


def shards(offsets, fractions, masses, cotangents, counts):
    width_x, width_y, depth = masses.shape
    raw = deposit(offsets, fractions, masses, cotangents, counts)
    below = from_behind(raw[:, :, width_y + 7 : width_y + 17], "gy", 1)
    above = from_behind(raw[:, :, 7:17], "gy", -1)
    rows = raw[:, :, 7 : width_y + 17]
    pad = ((0, 0), (0, 0), (0, width_y), (0, 0)), ((0, 0), (0, 0), (width_y, 0), (0, 0))
    rows = rows + jnp.pad(below, pad[0]) + jnp.pad(above, pad[1])
    density = rows[0]
    adjoint = rows[1, :, 1 : width_y + 9]
    density = join_x(density, *send_x(density, width_x, 0, 1), width_x, 0, 1)
    adjoint = join_x(adjoint, *send_x(adjoint, width_x, 1, 0), width_x, 1, 0)
    force_x = -0.5 * (density[2:, 1:-1] - density[:-2, 1:-1])
    force_y = -0.5 * (density[1:-1, 2:] - density[1:-1, :-2])
    force_z = -0.5 * (jnp.roll(density, -1, 2) - jnp.roll(density, 1, 2))[1:-1, 1:-1]
    return jnp.stack([force_x, force_y, force_z]), adjoint[1:-1]


def solution(mesh):
    in_specs = (
        P("groups", "gx", "gy", None),
        P("groups", "gx", "gy", None),
        P("gx", "gy", "groups"),
        P("groups", "gx", "gy", None),
        P(("groups", "gx"), "gy"),
    )
    out_specs = (P("groups", "gx", "gy", None), P(("groups", "gx"), "gy", None))
    return jax.shard_map(shards, mesh=mesh, in_specs=in_specs, out_specs=out_specs, check_vma=False)
```

```python
import functools

import jax
import jax.numpy as jnp
from jax import lax
from jax.experimental import pallas as pl
from jax.experimental.pallas import tpu as pltpu
from jax.sharding import PartitionSpec as P

TROWS = 8
REACH = 9
WINDOW = 16
PAIR = 2
EDGE = 8


def deposit_kernel(counts_ref, off_ref, frac_ref, mass_ref, cot_ref, out_ref, mesh, prep, left, right):
    x = pl.program_id(0)
    width_y, depth = mass_ref.shape[1:]
    planes, rows_all = mesh.shape[1:3]
    span = PAIR * depth

    @pl.when(x == 0)
    def _():
        mesh[...] = jnp.zeros_like(mesh)

    sub = lax.broadcasted_iota(jnp.int32, (TROWS, depth), 0)
    lane = lax.broadcasted_iota(jnp.int32, (TROWS, depth), 1)
    window_y = lax.broadcasted_iota(jnp.int32, (WINDOW, depth), 0).astype(jnp.float32)
    window_z = lax.broadcasted_iota(jnp.int32, (depth, depth), 0).astype(jnp.float32).astype(jnp.bfloat16)
    zero16 = jnp.zeros((depth, depth), jnp.bfloat16)

    def spread(index, row, count):
        return jnp.broadcast_to(prep[index, row : row + 1, :], (count, depth))

    def build(pair):
        for row in range(PAIR * pair, PAIR * pair + PAIR):
            cols = slice(row * depth, row * depth + depth)
            cell = spread(13, row, WINDOW)
            upper = spread(14, row, WINDOW)
            weight_y = jnp.where(
                window_y == cell, 1.0 - upper, jnp.where(window_y == cell + 1.0, upper, 0.0)
            )
            tops = [weight_y * spread(9 + k, row, WINDOW) for k in range(4)]
            for dx in range(REACH):
                weight_x = spread(dx, row, WINDOW)
                for k in range(4):
                    at = (k * REACH + dx) * WINDOW
                    left[at : at + WINDOW, cols] = (weight_x * tops[k]).astype(jnp.bfloat16)
            low = spread(15, row, depth).astype(jnp.bfloat16)
            high = spread(16, row, depth).astype(jnp.bfloat16)
            one = spread(17, row, depth).astype(jnp.bfloat16)
            two = spread(18, row, depth).astype(jnp.bfloat16)
            right[:, cols] = jnp.where(
                window_z == low, one, jnp.where(window_z == high, two, zero16)
            )

    def tile(t, carry):
        rows = pl.ds(pl.multiple_of(t * TROWS, TROWS), TROWS)
        count = counts_ref[x, t]
        live = sub * depth + lane < count
        shift_x = off_ref[0, 0, rows, :] + 4
        frac_x = frac_ref[0, 0, rows, :]
        for dx in range(REACH):
            prep[dx] = jnp.where(
                shift_x == dx, 1.0 - frac_x, jnp.where(shift_x == dx - 1, frac_x, 0.0)
            )
        prep[9] = jnp.where(live, mass_ref[0, rows, :], 0.0)
        for k in range(3):
            prep[10 + k] = jnp.where(live, cot_ref[k, 0, rows, :], 0.0)
        prep[13] = (off_ref[1, 0, rows, :] + sub + 4).astype(jnp.float32)
        prep[14] = frac_ref[1, 0, rows, :]
        lower = lane + off_ref[2, 0, rows, :]
        prep[15] = ((lower + depth) % depth).astype(jnp.float32)
        prep[16] = ((lower + (depth + 1)) % depth).astype(jnp.float32)
        frac_z = frac_ref[2, 0, rows, :]
        prep[17] = 1.0 - frac_z
        prep[18] = frac_z

        def work(pairs):
            for pair in range(pairs):
                build(pair)
            product = lax.dot_general(
                left[:, : pairs * span],
                right[:, : pairs * span],
                (((1,), (1,)), ((), ())),
                preferred_element_type=jnp.float32,
            ).reshape(4, REACH, WINDOW, depth)
            place = (slice(None), pl.ds(x + 2, REACH), pl.ds(pl.multiple_of(t * TROWS + EDGE, TROWS), WINDOW), slice(None))
            mesh[place] = mesh[place] + product

        most = TROWS // PAIR
        for pairs in range(1, most + 1):
            @pl.when((count > span * (pairs - 1)) & (count <= span * pairs))
            def _():
                work(pairs)

        return carry

    lax.fori_loop(0, width_y // TROWS, tile, 0)

    @pl.when(x == pl.num_programs(0) - 1)
    def _():
        def finish(p, carry):
            out_ref[0, p] = mesh[0, p + 1]
            side = mesh[2, p + 1]
            along = mesh[3, p + 1]
            out_ref[1, p] = 0.5 * (
                (mesh[1, p + 2] - mesh[1, p])
                + (pltpu.roll(side, rows_all - 1, 0) - pltpu.roll(side, 1, 0))
                + (pltpu.roll(along, depth - 1, 1) - pltpu.roll(along, 1, 1))
            )
            return carry

        lax.fori_loop(0, planes - 2, finish, 0)


def deposit(offsets, fractions, masses, cotangents, counts):
    width_x, width_y, depth = masses.shape
    rows_all = width_y + 8 + 2 * EDGE
    planes = width_x + 12
    triple = pl.BlockSpec((3, 1, width_y, depth), lambda i: (0, i, 0, 0))
    return pl.pallas_call(
        deposit_kernel,
        grid=(width_x,),
        out_shape=jax.ShapeDtypeStruct((2, planes - 2, rows_all, depth), jnp.float32),
        in_specs=[
            pl.BlockSpec(memory_space=pltpu.SMEM),
            triple,
            triple,
            pl.BlockSpec((1, width_y, depth), lambda i: (i, 0, 0)),
            triple,
        ],
        out_specs=pl.BlockSpec((2, planes - 2, rows_all, depth), lambda i: (0, 0, 0, 0)),
        scratch_shapes=[
            pltpu.VMEM((4, planes, rows_all, depth), jnp.float32),
            pltpu.VMEM((19, TROWS, depth), jnp.float32),
            pltpu.VMEM((4 * REACH * WINDOW, TROWS * depth), jnp.bfloat16),
            pltpu.VMEM((depth, TROWS * depth), jnp.bfloat16),
        ],
        compiler_params=pltpu.CompilerParams(vmem_limit_bytes=56 << 20),
        name="deposit",
    )(counts, offsets, fractions, masses, cotangents)


def from_behind(block, axis, distance):
    devices = range(lax.axis_size(axis))
    route = [((i - distance) % len(devices), i) for i in devices]
    return lax.ppermute(block, axis, route)


def send_x(field, width_x, low, high):
    behind = from_behind(field[width_x + low : width_x + low + 9], "gx", 1)
    ahead = from_behind(field[high : high + 9], "gx", -1)
    return behind, ahead


def join_x(field, behind, ahead, width_x, low, high):
    return (
        field
        + jnp.pad(behind, ((low, width_x + 1 - low), (0, 0), (0, 0)))
        + jnp.pad(ahead, ((width_x + high, 1 - high), (0, 0), (0, 0)))
    )


def shards(offsets, fractions, masses, cotangents, counts):
    width_x, width_y, depth = masses.shape
    raw = deposit(offsets, fractions, masses, cotangents, counts)
    below = from_behind(raw[:, :, width_y + 7 : width_y + 17], "gy", 1)
    above = from_behind(raw[:, :, 7:17], "gy", -1)
    rows = raw[:, :, 7 : width_y + 17]
    pad = ((0, 0), (0, 0), (0, width_y), (0, 0)), ((0, 0), (0, 0), (width_y, 0), (0, 0))
    rows = rows + jnp.pad(below, pad[0]) + jnp.pad(above, pad[1])
    density = rows[0]
    adjoint = rows[1, :, 1 : width_y + 9]
    density = join_x(density, *send_x(density, width_x, 0, 1), width_x, 0, 1)
    adjoint = join_x(adjoint, *send_x(adjoint, width_x, 1, 0), width_x, 1, 0)
    force_x = -0.5 * (density[2:, 1:-1] - density[:-2, 1:-1])
    force_y = -0.5 * (density[1:-1, 2:] - density[1:-1, :-2])
    force_z = -0.5 * (jnp.roll(density, -1, 2) - jnp.roll(density, 1, 2))[1:-1, 1:-1]
    return jnp.stack([force_x, force_y, force_z]), adjoint[1:-1]


def solution(mesh):
    in_specs = (
        P("groups", "gx", "gy", None),
        P("groups", "gx", "gy", None),
        P("gx", "gy", "groups"),
        P("groups", "gx", "gy", None),
        P(("groups", "gx"), "gy"),
    )
    out_specs = (P("groups", "gx", "gy", None), P(("groups", "gx"), "gy", None))
    return jax.shard_map(shards, mesh=mesh, in_specs=in_specs, out_specs=out_specs, check_vma=False)
```
